32 devices in a mesh: groups: 2 (over y), space: 4 (over z), date: 2 (over x), band: 2 (over core).
Axes of the slice: x: 2, y: 2, z: 4, core: 2. Of those that a mesh axis runs over, the one named last changes fastest.
Arguments:
- reflect: float32 [16, 8, 256, 256], P('date', 'band', ('groups', 'space')), parts along dimension 2, may hold values from -6 to 6
- kernels: float32 [3, 8, 33], P(None, 'band'), may hold values from 0.2 to 2
- strength: float32 [3, 8], P(None, 'band'), may hold values from 0.2 to 0.6
- destinations: int32 [128, 1], P(('groups', 'space')), parts along dimension 0, may hold values from 0 to 3; in each aligned block of 16 rows (0 to 15, 16 to 31, ...) at most 8 rows name the same one
- offsets: int32 [128], P(('groups', 'space')), parts along dimension 0, may hold values from 0 to 60
- counts: int32 [16, 8], P('date', ('groups', 'space')), parts along dimension 1, may hold values from 1 to 8192
- resample_rows: float32 [8, 4, 4], P(('groups', 'space')), parts along dimension 0, may hold values from -3 to 3
- resample_columns: float32 [8, 128, 128], P(('groups', 'space')), parts along dimension 0, may hold values from -0.5 to 0.5
Outputs:
- geomedian: float32 [8, 512, 128], P('band', ('groups', 'space')), parts along dimension 1
The draws below stay inside these ranges and needn't reach their ends.
There are 2 independent parts, one for each index of `groups`. The reference program is written for one: setup_inputs(seed, part) draws one part's arguments, and reference() takes and returns one part's arrays. A program takes and returns all parts, laid end to end along the dimension named above; an argument that names none is the same for every part. Nothing has to cross between parts.
Inputs may be any that keep to these rules, and one draw needn't show every extreme that they name: `destinations`: in each aligned block of 16 entries (the blocks of one strip) no tile is named more than 8 times, a bound that some block reaches.
All inputs are finite; a program needn't handle non-finite values.
Results may differ from the reference program's by a relative error of at most 0.00011.
Values sent between devices are 32-bit elements; how exact they have to be, the bound alone decides.
A program may use at most 128 MiB of HBM per device.

```python
import math
import jax
import jax.numpy as jnp
import numpy as np
from jax import lax

COLS = 256
BANDS = 8
PASSES = 3
RADIUS = 16
BROWS = 4
BCOLS = 128
ITERS = 4
TAPS = 33
DATES = 16
ROWS = 128
NCB = 2
NBLK_DEV = 16
NBLK = 64
TILES = 4
TROWS = 64
MROWS = 256
MOST = 8


def touch_ends(entries, rng, smallest, largest):
    longest = entries.shape.index(max(entries.shape))
    spots = []
    for shift in (0, 1):
        where = [jax.random.randint(jax.random.fold_in(rng, axis), (), 0, length) for axis, length in enumerate(entries.shape)]
        where[longest] = (where[longest] + shift) % entries.shape[longest]
        spots.append(tuple(where))
    return entries.at[spots[0]].set(smallest).at[spots[1]].set(largest)


def levels(key, dims, split, low, largest):
    level, own = 1.0, jax.random.fold_in(key, 6)
    for dim, shards_of in split:
        heights = jnp.exp(jax.random.uniform(jax.random.fold_in(own, dim), (shards_of,), jnp.float32, low / len(split), largest / len(split)))
        level = level * jnp.repeat(heights, dims[dim] // shards_of).reshape([-1 if axis == dim else 1 for axis in range(len(dims))])
    return level


def assign_block(own_key, own, number, rows, number_of, top, reach, skew):
    ranking = jax.random.permutation(own_key, number_of)
    packed, ordinary = load_shares(number_of, rows * top, reach, skew, True), load_shares(number_of, rows * top, reach, skew, False)
    places = jnp.arange(number_of)

    def named(lengths, turn):
        used = int((lengths > 0).sum())
        fixed = max(1, used // 4)
        moved = fixed + (places - fixed + turn * (used - fixed)) % max(1, number_of - fixed)
        return jnp.zeros((number_of,), jnp.int32).at[ranking[jnp.where(places < fixed, places, moved)]].set(jnp.asarray(lengths, jnp.int32))

    lengths = jnp.where(number % 4 == 0, named(packed, number // 4), named(ordinary, number - number // 4 - 1))
    mixed = jax.random.permutation(jax.random.fold_in(own, 3), number_of)
    giver, receiver = mixed[0:number_of // 2 * 2:2], mixed[1:number_of // 2 * 2:2]
    room = jnp.minimum(lengths[giver] - 1, reach - lengths[receiver]) // 2
    room = jnp.where((giver == ranking[0]) | (receiver == ranking[0]) | (lengths[receiver] == 0), 0, jnp.maximum(room, 0))
    moved = jax.random.randint(jax.random.fold_in(own, 4), (number_of // 2,), 0, 1 << 20) % (room + 1)
    lengths = lengths.at[giver].add(-moved).at[receiver].add(moved)
    members = jnp.searchsorted(jnp.cumsum(lengths), jnp.arange(rows * top), side="right").astype(jnp.int32)
    table = members.reshape(top, rows).T
    table = table[jax.random.permutation(jax.random.fold_in(own, 1), rows)]
    turn = jax.random.randint(jax.random.fold_in(own, 2), (rows, 1), 0, top)
    return jnp.take_along_axis(table, (jnp.arange(top)[None, :] + turn) % top, axis=1)


def load_shares(amount, total, most, skew, full):
    loads = [(1 << 20) // math.isqrt(grade ** skew) + 1 for grade in range(1, amount + 1)]
    largest = most if full else min(most, max(-(-total // amount), total * loads[0] // sum(loads)))
    least = 1 if total - largest >= amount - 1 else 0
    holding, rest = [largest] + [least] * (amount - 1), total - largest - least * (amount - 1)
    while rest > 0:
        movable = [i for i in range(1, amount) if holding[i] < largest] or [i for i in range(1, amount) if holding[i] < most]
        whole, left = sum([loads[i] for i in movable]), rest
        for i in movable:
            more = min(most - holding[i], max(1, left * loads[i] // whole), rest)
            holding[i] = holding[i] + more
            rest = rest - more
    return np.array(holding)


def bell_draw(rng, shape, width, bound, split=(), kind=jnp.bfloat16):
    loudness = levels(rng, shape, split, -0.22, 0.18) if split else 1.0
    result = jax.random.normal(rng, shape, jnp.float32) * width * loudness
    return jnp.minimum(jnp.maximum(result, -bound), bound).astype(kind)


def setup_inputs(seed: int = 0, part: int = 0) -> dict:
    streams_of = jax.random.split(jax.random.key(seed), 9)
    part_splits = jax.random.split(jax.random.fold_in(streams_of[8], part), 9)
    reflect = bell_draw(part_splits[0], (DATES, BANDS, ROWS, COLS), 1.0, 6.0, ((0, 2), (1, 2), (2, 4)), jnp.float32)
    kernels = jnp.clip(jnp.exp(math.log(2.0) - 2.3025851 * jax.random.uniform(streams_of[1], (PASSES, BANDS, TAPS), jnp.float32) ** levels(streams_of[1], (PASSES, BANDS, TAPS), ((1, 2),), -0.2, 0.2)), 0.2, 2.0)
    strength = jnp.clip(0.2 + 0.400000021 * jax.random.uniform(streams_of[2], (PASSES, BANDS), jnp.float32) ** levels(streams_of[2], (PASSES, BANDS), ((1, 2),), -0.2, 0.2), 0.2, 0.6)
    destinations_keys = jax.random.split(jax.random.fold_in(part_splits[3], 1), NBLK // NBLK_DEV)
    destinations_turns = jax.random.permutation(jax.random.fold_in(part_splits[3], 3), NBLK // NBLK_DEV)
    destinations = jax.vmap(lambda own, number: assign_block(jax.random.fold_in(part_splits[3], 2), own, number, NBLK_DEV, TILES, 1, MOST, 2))(destinations_keys, destinations_turns).reshape((NBLK, 1))
    offsets = touch_ends(jax.random.randint(part_splits[4], (NBLK,), 0, TROWS - BROWS + 1), jax.random.fold_in(part_splits[4], 1), 0, TROWS - BROWS).astype(jnp.int32)
    counts = touch_ends(jax.random.randint(part_splits[5], (DATES, TILES), 1, TROWS * BCOLS + 1), jax.random.fold_in(part_splits[5], 1), 1, TROWS * BCOLS).astype(jnp.int32)
    resample_rows = bell_draw(part_splits[6], (TILES, BROWS, BROWS), BROWS ** -0.5, 3.0, ((0, 4),), jnp.float32)
    resample_columns = bell_draw(part_splits[7], (TILES, BCOLS, BCOLS), BCOLS ** -0.5, 0.5, ((0, 4),), jnp.float32)
    return {"reflect": reflect, "kernels": kernels, "strength": strength, "destinations": destinations, "offsets": offsets, "counts": counts, "resample_rows": resample_rows, "resample_columns": resample_columns}


highest = lax.Precision.HIGHEST
smooth_sq = 0.01

def band_matrix(weights, count_out, count_in, lead_shift):
    tap_count = weights.shape[1]
    offset = jnp.arange(count_in)[None, :] - jnp.arange(count_out)[:, None] + lead_shift
    matrix = jnp.zeros((weights.shape[0], count_out, count_in), jnp.float32)
    for tap_index in range(tap_count):
        chosen = (offset == tap_index).astype(jnp.float32)
        matrix = matrix + weights[:, tap_index, None, None] * chosen[None, :, :]
    return matrix

def reference(reflect, kernels, strength, destinations, offsets, counts, resample_rows, resample_columns):
    values = reflect
    for pass_index in range(PASSES):
        norm_taps = kernels[pass_index] / lax.optimization_barrier(jnp.sum(kernels[pass_index], axis=1, keepdims=True))
        row_matrix = band_matrix(norm_taps, ROWS, ROWS, RADIUS)
        column_matrix = band_matrix(norm_taps, COLS, COLS, RADIUS)
        row_pass = jnp.einsum('bij,tbjc->tbic', row_matrix, values, precision=highest)
        blurred = jnp.einsum('tbrj,bcj->tbrc', row_pass, column_matrix, precision=highest)
        values = values + strength[pass_index][None, :, None, None] * (values - blurred)
    shaped = values.reshape(DATES, BANDS, ROWS // BROWS, BROWS, NCB, BCOLS)
    blocks = shaped.transpose(2, 4, 0, 1, 3, 5).reshape(NBLK, DATES, BANDS, BROWS, BCOLS)
    targets = destinations[:, 0]
    block_rows = resample_rows[targets]
    block_columns = resample_columns[targets]
    row_pass = jnp.einsum('nij,ntbjc->ntbic', block_rows, blocks, precision=highest)
    resampled = jnp.einsum('ntbic,ncv->ntbiv', row_pass, block_columns, precision=highest)
    map_row = targets[:, None] * TROWS + offsets[:, None] + jnp.arange(BROWS, dtype=jnp.int32)[None, :]
    flat_rows = resampled.transpose(0, 3, 1, 2, 4).reshape(NBLK * BROWS, DATES, BANDS, BCOLS)
    assembled = jax.ops.segment_sum(flat_rows, map_row.reshape(-1).astype(jnp.int32), num_segments=MROWS)
    stacked = assembled.transpose(1, 2, 0, 3).reshape(DATES, BANDS, MROWS * BCOLS)
    count_values = counts.astype(jnp.float32)
    mean_count = jnp.sum(count_values) / (DATES * TILES)
    weight_tile = count_values / (count_values + mean_count)
    weight_pixel = jnp.repeat(weight_tile, TROWS * BCOLS, axis=1)
    numerator = lax.optimization_barrier(jnp.sum(weight_pixel[:, None, :] * stacked, axis=0))
    denominator = lax.optimization_barrier(jnp.sum(weight_pixel, axis=0))
    estimate = numerator / denominator[None, :]
    for iter_index in range(ITERS):
        distance = jnp.sqrt(lax.optimization_barrier(jnp.sum((stacked - estimate[None]) ** 2, axis=1)) + smooth_sq)
        scaled = weight_pixel / distance
        numerator = lax.optimization_barrier(jnp.sum(scaled[:, None, :] * stacked, axis=0))
        denominator = lax.optimization_barrier(jnp.sum(scaled, axis=0))
        estimate = numerator / denominator[None, :]
    return estimate.reshape(BANDS, MROWS, BCOLS)
```

```python
import functools
import jax
import jax.numpy as jnp
from jax import lax
from jax.experimental import pallas as pl
from jax.experimental.pallas import tpu as pltpu
from jax.sharding import PartitionSpec as P

BROWS = 4
BCOLS = 128
ITERS = 4
MESH = pl.DeviceIdType.MESH
smooth_sq = 0.01
f32 = jnp.float32
bf16 = jnp.bfloat16


def split(value):
    high = value.astype(bf16)
    return high, (value - high.astype(f32)).astype(bf16)


def dot3(left, right):
    lh, ll = left
    rh, rl = right
    d = functools.partial(jnp.dot, preferred_element_type=f32)
    return d(lh, rh) + (d(ll, rh) + d(lh, rl))


def toeplitz(row, size, radius):
    base = jnp.broadcast_to(row, (8, size))
    base = pltpu.roll(base, size - radius, 1)
    sub = lax.broadcasted_iota(jnp.int32, (8, size), 0)
    for bit in (1, 2, 4):
        base = jnp.where((sub & bit) != 0, pltpu.roll(base, bit, 1), base)
    gap = lax.broadcasted_iota(jnp.int32, (8, size), 1) - sub
    parts = []
    for start in range(0, size, 8):
        turned = base if start == 0 else pltpu.roll(base, start, 1)
        near = jnp.abs(gap - start) <= radius
        parts.append(jnp.where(near, turned, 0.0))
    return jnp.concatenate(parts, axis=0)


def kernel(
    dims, x_ref, meta_ref, taps_ref, strength_ref, cols_ref, out_ref,
    grid, row_h, row_l, col_h, col_l, meta_all, place_h, place_l, asm, stack, est, res,
    msend, mrecv, gsend, grecv, ssend, srecv, esend, erecv,
):
    S, D, C, T, B, RS, W, PASSES, radius, ppd, nch = dims
    n = S * D * C
    rows = S * RS
    nb = min(B, ppd)
    cp = ppd // nch
    share = asm.shape[2]
    s = lax.axis_index("space")
    d = lax.axis_index("date")
    c = lax.axis_index("band")
    me = (s * D + d) * C + c
    dc = d * C + c
    q0 = s * ppd

    def where_is(index):
        return {
            "space": index // (D * C),
            "date": lax.rem(index // C, D),
            "band": lax.rem(index, C),
        }

    barrier = pltpu.get_barrier_semaphore()

    def greet(k, carry):
        other = lax.rem(me + k, n)
        pl.semaphore_signal(barrier, inc=1, device_id=where_is(other), device_id_type=MESH)
        return carry

    lax.fori_loop(1, n, greet, 0)
    pl.semaphore_wait(barrier, n - 1)

    md = s * D + d

    def meta_copy(to, slot, sem):
        return pltpu.make_async_remote_copy(
            src_ref=meta_ref,
            dst_ref=meta_all.at[slot],
            send_sem=msend.at[to],
            recv_sem=mrecv.at[sem],
            device_id={"space": to // D, "date": lax.rem(to, D)},
            device_id_type=MESH,
        )

    def meta_start(k, carry):
        meta_copy(lax.rem(md + k, S * D), md, md).start()
        return carry

    lax.fori_loop(1, S * D, meta_start, 0)
    meta_all[md] = meta_ref[...]

    def grid_copy(other, chunk, at):
        return pltpu.make_async_remote_copy(
            src_ref=x_ref.at[pl.ds(other * ppd + chunk * cp, cp)],
            dst_ref=grid.at[pl.ds(chunk * cp, cp), pl.ds(pl.multiple_of(at * RS, RS), RS)],
            send_sem=gsend.at[other, chunk],
            recv_sem=grecv.at[at, chunk],
            device_id={"space": other},
            device_id_type=MESH,
        )

    for chunk in range(nch):

        def grid_start(k, carry, chunk=chunk):
            grid_copy(lax.rem(s + k, S), chunk, s).start()
            return carry

        lax.fori_loop(1, S, grid_start, 0)
    grid[:, pl.ds(pl.multiple_of(s * RS, RS), RS), :] = x_ref[pl.ds(q0, ppd)]

    def build(index, carry):
        which = index // nb
        local_band = lax.rem(index, nb)
        band = lax.rem(q0 + local_band, B)
        both = taps_ref[which * B + band]
        both = both / jnp.sum(both, axis=1, keepdims=True)
        high, low = split(toeplitz(both[0:1, :rows], rows, radius))
        row_h[index] = high
        row_l[index] = low
        high, low = split(toeplitz(both[1:2, :W], W, radius))
        col_h[index] = high
        col_l[index] = low
        return carry

    lax.fori_loop(0, PASSES * nb, build, 0)

    def meta_wait(k, carry):
        other = lax.rem(md + k, S * D)
        copy = meta_copy(other, other, other)
        copy.wait_send()
        copy.wait_recv()
        return carry

    lax.fori_loop(1, S * D, meta_wait, 0)

    tile_rows = share * D * C
    pieces = [meta_all[i * D + d, 0:8, :] for i in range(S)]
    total = pieces[0]
    for piece in pieces[1:]:
        total = total + piece
    map_row = lax.broadcasted_iota(jnp.int32, (S * tile_rows, rows), 0)
    for half in range(2):
        target = total[half : half + 1]
        first = total[2 + half : 3 + half].astype(jnp.int32)
        behind = map_row - first
        place = jnp.zeros((S * tile_rows, rows), f32)
        for i in range(BROWS):
            value = jnp.zeros((1, rows), f32)
            for tile in range(S):
                value = value + jnp.where(target == tile, pieces[tile][4 + i : 5 + i], 0.0)
            place = jnp.where(behind == i, value, place)
        high, low = split(place)
        place_h[half] = high
        place_l[half] = low

    def share_copy(other, source, chunk):
        sd = lax.rem(source // C, D)
        sc = lax.rem(source, C)
        ss = source // (D * C)
        return pltpu.make_async_remote_copy(
            src_ref=asm.at[other, pl.ds(chunk * cp, cp)],
            dst_ref=stack.at[sd, sc, pl.ds(ss * ppd + chunk * cp, cp)],
            send_sem=ssend.at[other, chunk],
            recv_sem=srecv.at[source, chunk],
            device_id=where_is(other),
            device_id_type=MESH,
        )

    def chunk_step(chunk, carry):
        def grid_wait(k, inner):
            other = lax.rem(s + k, S)
            grid_copy(other, chunk, other).wait_recv()
            return inner

        lax.fori_loop(1, S, grid_wait, 0)
        for j in range(cp):
            plane = chunk * cp + j
            local_band = lax.rem(plane, nb)
            band = lax.rem(q0 + plane, B)
            value = grid[plane]
            for which in range(PASSES):
                index = which * nb + local_band
                mid = dot3((row_h[index], row_l[index]), split(value))
                blurred = dot3(split(mid), (col_h[index], col_l[index]))
                value = value + strength_ref[which, band] * (value - blurred)
            vh, vl = split(value)
            laid = dot3((place_h[0], place_l[0]), (vh[:, :BCOLS], vl[:, :BCOLS]))
            laid = laid + dot3((place_h[1], place_l[1]), (vh[:, BCOLS:], vl[:, BCOLS:]))
            asm[:, plane] = laid.reshape(n, share, BCOLS)

        def share_start(k, inner):
            share_copy(lax.rem(me + k, n), me, chunk).start()
            return inner

        lax.fori_loop(1, n, share_start, 0)
        return carry

    lax.fori_loop(0, nch, chunk_step, 0)
    stack[d, c, pl.ds(q0, ppd)] = asm[me]

    col_pair = split(cols_ref[...])

    def resample(source):
        sd = lax.rem(source // C, D)
        sc = lax.rem(source, C)
        ss = source // (D * C)
        block = stack[sd, sc, pl.ds(ss * ppd, ppd)].reshape(ppd * share, BCOLS)
        done = dot3(split(block), col_pair)
        stack[sd, sc, pl.ds(ss * ppd, ppd)] = done.reshape(ppd, share, BCOLS)

    resample(me)

    def share_wait(k, carry):
        source = lax.rem(me + n - k, n)

        def one(chunk, inner):
            share_copy(me, source, chunk).wait_recv()
            return inner

        lax.fori_loop(0, nch, one, 0)
        resample(source)
        return carry

    lax.fori_loop(1, n, share_wait, 0)

    count_sum = jnp.zeros((1, BCOLS), f32)
    for i in range(S * D):
        count_sum = count_sum + jnp.sum(meta_all[i, 8 : 8 + T, :BCOLS], axis=0, keepdims=True)
    mean_count = count_sum / (T * D * S)
    weights = []
    for i in range(D):
        mine = meta_all[s * D + i, 8 : 8 + T, :BCOLS]
        weights.append(mine / (mine + mean_count))

    step = 8 if share % 8 == 0 else share
    for start in range(0, share, step):

        def picked(i, t):
            return stack[i, :, t * B : (t + 1) * B, start : start + step, :]

        def weighted(estimate):
            num = jnp.zeros((C, B, step, BCOLS), f32)
            den = jnp.zeros((step, BCOLS), f32)
            for i in range(D):
                for t in range(T):
                    part = picked(i, t)
                    weight = jnp.broadcast_to(weights[i][t : t + 1], (step, BCOLS))
                    if estimate is not None:
                        away = part - estimate
                        square = jnp.sum(jnp.sum(away * away, axis=0), axis=0)
                        weight = weight * lax.rsqrt(square + smooth_sq)
                    num = num + weight * part
                    den = den + weight
            return num / den

        estimate = weighted(None)
        estimate = lax.fori_loop(0, ITERS, lambda _, e: weighted(e), estimate)
        est[:, :, start : start + step, :] = estimate

    def est_copy(other, source):
        return pltpu.make_async_remote_copy(
            src_ref=est.at[lax.rem(other, C)],
            dst_ref=res.at[source],
            send_sem=esend.at[other],
            recv_sem=erecv.at[source],
            device_id={"date": other // C, "band": lax.rem(other, C)},
            device_id_type=MESH,
        )

    def est_start(k, carry):
        est_copy(lax.rem(dc + k, D * C), dc).start()
        return carry

    lax.fori_loop(1, D * C, est_start, 0)
    res[dc] = est[c]

    def est_wait(k, carry):
        other = lax.rem(dc + k, D * C)
        copy = est_copy(other, other)
        copy.wait_send()
        copy.wait_recv()
        return carry

    lax.fori_loop(1, D * C, est_wait, 0)
    for i in range(D * C):
        out_ref[:, i * share : (i + 1) * share, :] = res[i]

    def chunk_end(chunk, carry):
        def grid_end(k, inner):
            grid_copy(lax.rem(s + k, S), chunk, s).wait_send()
            return inner

        def share_end(k, inner):
            share_copy(lax.rem(me + k, n), me, chunk).wait_send()
            return inner

        lax.fori_loop(1, S, grid_end, 0)
        lax.fori_loop(1, n, share_end, 0)
        return carry

    lax.fori_loop(0, nch, chunk_end, 0)


def local(
    reflect, kernels, strength, destinations, offsets, counts, resample_rows, resample_columns
):
    S, D, C = lax.axis_size("space"), lax.axis_size("date"), lax.axis_size("band")
    T, B, RS, W = reflect.shape
    PASSES, _, tap_count = kernels.shape
    radius = (tap_count - 1) // 2
    rows = S * RS
    n = S * D * C
    ppd = T * B // S
    nch = min(4, ppd)
    nb = min(B, ppd)
    tile_rows = destinations.shape[0] * BROWS
    share = tile_rows // (D * C)
    s = lax.axis_index("space")

    target = destinations[:, 0].reshape(-1, 2).T
    first = target * tile_rows + offsets.reshape(-1, 2).T
    places = jnp.repeat(jnp.concatenate([target, first]), BROWS, axis=1)
    strip = jnp.arange(rows)[None, :] // RS == s
    places = jnp.where(strip, jnp.tile(places, (1, S)), 0).astype(f32)
    tiled_rows = jnp.tile(resample_rows[0], (1, rows // BROWS))
    meta = jnp.concatenate(
        [places, tiled_rows, jnp.broadcast_to(counts.astype(f32), (T, rows))]
    )
    width = max(W, rows)
    taps = jnp.stack([kernels, kernels[:, :, ::-1]], axis=2).reshape(PASSES * B, 2, tap_count)
    taps = jnp.pad(taps, ((0, 0), (0, 0), (0, width - tap_count)))

    dims = (S, D, C, T, B, RS, W, PASSES, radius, ppd, nch)
    vmem = pl.BlockSpec(memory_space=pltpu.VMEM)
    smem = pl.BlockSpec(memory_space=pltpu.SMEM)
    dma = pltpu.SemaphoreType.DMA
    return pl.pallas_call(
        functools.partial(kernel, dims),
        out_shape=jax.ShapeDtypeStruct((B, tile_rows, BCOLS), f32),
        in_specs=[vmem, vmem, vmem, smem, vmem],
        out_specs=vmem,
        scratch_shapes=[
            pltpu.VMEM((ppd, rows, W), f32),
            pltpu.VMEM((PASSES * nb, rows, rows), bf16),
            pltpu.VMEM((PASSES * nb, rows, rows), bf16),
            pltpu.VMEM((PASSES * nb, W, W), bf16),
            pltpu.VMEM((PASSES * nb, W, W), bf16),
            pltpu.VMEM((S * D, 8 + T, rows), f32),
            pltpu.VMEM((2, S * tile_rows, rows), bf16),
            pltpu.VMEM((2, S * tile_rows, rows), bf16),
            pltpu.VMEM((n, ppd, share, BCOLS), f32),
            pltpu.VMEM((D, C, T * B, share, BCOLS), f32),
            pltpu.VMEM((C, B, share, BCOLS), f32),
            pltpu.VMEM((D * C, B, share, BCOLS), f32),
            dma((S * D,)),
            dma((S * D,)),
            dma((S, nch)),
            dma((S, nch)),
            dma((n, nch)),
            dma((n, nch)),
            dma((D * C,)),
            dma((D * C,)),
        ],
        compiler_params=pltpu.CompilerParams(
            collective_id=0, has_side_effects=True, vmem_limit_bytes=56 * 1024 * 1024
        ),
    )(reflect.reshape(T * B, RS, W), meta, taps, strength, resample_columns[0])


def solution(mesh):
    in_specs = (
        P("date", "band", ("groups", "space"), None),
        P(None, "band", None),
        P(None, "band"),
        P(("groups", "space"), None),
        P(("groups", "space")),
        P("date", ("groups", "space")),
        P(("groups", "space"), None, None),
        P(("groups", "space"), None, None),
    )
    out_specs = P("band", ("groups", "space"), None)
    return jax.shard_map(local, mesh=mesh, in_specs=in_specs, out_specs=out_specs, check_vma=False)
```

```python
import functools
import jax
import jax.numpy as jnp
from jax import lax
from jax.experimental import pallas as pl
from jax.experimental.pallas import tpu as pltpu
from jax.sharding import PartitionSpec as P

BROWS = 4
BCOLS = 128
ITERS = 4
MESH = pl.DeviceIdType.MESH
smooth_sq = 0.01
f32 = jnp.float32
bf16 = jnp.bfloat16


def split(value):
    high = value.astype(bf16)
    return high, (value - high.astype(f32)).astype(bf16)


def dot3(left, right):
    lh, ll = left
    rh, rl = right
    d = functools.partial(jnp.dot, preferred_element_type=f32)
    return d(lh, rh) + (d(ll, rh) + d(lh, rl))


def toeplitz(row, size, radius):
    base = jnp.broadcast_to(row, (8, size))
    base = pltpu.roll(base, size - radius, 1)
    sub = lax.broadcasted_iota(jnp.int32, (8, size), 0)
    for bit in (1, 2, 4):
        base = jnp.where((sub & bit) != 0, pltpu.roll(base, bit, 1), base)
    gap = lax.broadcasted_iota(jnp.int32, (8, size), 1) - sub
    parts = []
    for start in range(0, size, 8):
        turned = base if start == 0 else pltpu.roll(base, start, 1)
        near = jnp.abs(gap - start) <= radius
        parts.append(jnp.where(near, turned, 0.0))
    return jnp.concatenate(parts, axis=0)


def kernel(
    dims, x_ref, meta_ref, taps_ref, strength_ref, cols_ref, out_ref,
    grid, row_h, row_l, col_h, col_l, meta_all, place_h, place_l, asm, stack, est, res,
    msend, mrecv, gsend, grecv, ssend, srecv, esend, erecv,
):
    S, D, C, T, B, RS, W, PASSES, radius, ppd, nch = dims
    n = S * D * C
    rows = S * RS
    nb = min(B, ppd)
    cp = ppd // nch
    share = asm.shape[2]
    s = lax.axis_index("space")
    d = lax.axis_index("date")
    c = lax.axis_index("band")
    me = (s * D + d) * C + c
    dc = d * C + c
    q0 = s * ppd

    def where_is(index):
        return {
            "space": index // (D * C),
            "date": lax.rem(index // C, D),
            "band": lax.rem(index, C),
        }

    barrier = pltpu.get_barrier_semaphore()

    def greet(k, carry):
        other = lax.rem(me + k, n)
        pl.semaphore_signal(barrier, inc=1, device_id=where_is(other), device_id_type=MESH)
        return carry

    lax.fori_loop(1, n, greet, 0)
    pl.semaphore_wait(barrier, n - 1)

    md = s * D + d

    def meta_copy(to, slot, sem):
        return pltpu.make_async_remote_copy(
            src_ref=meta_ref,
            dst_ref=meta_all.at[slot],
            send_sem=msend.at[to],
            recv_sem=mrecv.at[sem],
            device_id={"space": to // D, "date": lax.rem(to, D)},
            device_id_type=MESH,
        )

    def meta_start(k, carry):
        meta_copy(lax.rem(md + k, S * D), md, md).start()
        return carry

    lax.fori_loop(1, S * D, meta_start, 0)
    meta_all[md] = meta_ref[...]

    def grid_copy(other, chunk, at):
        return pltpu.make_async_remote_copy(
            src_ref=x_ref.at[pl.ds(other * ppd + chunk * cp, cp)],
            dst_ref=grid.at[pl.ds(chunk * cp, cp), pl.ds(pl.multiple_of(at * RS, RS), RS)],
            send_sem=gsend.at[other, chunk],
            recv_sem=grecv.at[at, chunk],
            device_id={"space": other},
            device_id_type=MESH,
        )

    for chunk in range(nch):

        def grid_start(k, carry, chunk=chunk):
            grid_copy(lax.rem(s + k, S), chunk, s).start()
            return carry

        lax.fori_loop(1, S, grid_start, 0)
    grid[:, pl.ds(pl.multiple_of(s * RS, RS), RS), :] = x_ref[pl.ds(q0, ppd)]

    def build(index, carry):
        which = index // nb
        local_band = lax.rem(index, nb)
        band = lax.rem(q0 + local_band, B)
        both = taps_ref[which * B + band]
        both = both / jnp.sum(both, axis=1, keepdims=True)
        high, low = split(toeplitz(both[0:1, :rows], rows, radius))
        row_h[index] = high
        row_l[index] = low
        high, low = split(toeplitz(both[1:2, :W], W, radius))
        col_h[index] = high
        col_l[index] = low
        return carry

    lax.fori_loop(0, PASSES * nb, build, 0)

    def meta_wait(k, carry):
        other = lax.rem(md + k, S * D)
        copy = meta_copy(other, other, other)
        copy.wait_send()
        copy.wait_recv()
        return carry

    lax.fori_loop(1, S * D, meta_wait, 0)

    tile_rows = share * D * C
    pieces = [meta_all[i * D + d, 0:8, :] for i in range(S)]
    total = pieces[0]
    for piece in pieces[1:]:
        total = total + piece
    map_row = lax.broadcasted_iota(jnp.int32, (S * tile_rows, rows), 0)
    for half in range(2):
        target = total[half : half + 1]
        first = total[2 + half : 3 + half].astype(jnp.int32)
        behind = map_row - first
        place = jnp.zeros((S * tile_rows, rows), f32)
        for i in range(BROWS):
            value = jnp.zeros((1, rows), f32)
            for tile in range(S):
                value = value + jnp.where(target == tile, pieces[tile][4 + i : 5 + i], 0.0)
            place = jnp.where(behind == i, value, place)
        high, low = split(place)
        place_h[half] = high
        place_l[half] = low

    def share_copy(other, source, chunk):
        sd = lax.rem(source // C, D)
        sc = lax.rem(source, C)
        ss = source // (D * C)
        return pltpu.make_async_remote_copy(
            src_ref=asm.at[other, pl.ds(chunk * cp, cp)],
            dst_ref=stack.at[sd, sc, pl.ds(ss * ppd + chunk * cp, cp)],
            send_sem=ssend.at[other, chunk],
            recv_sem=srecv.at[source, chunk],
            device_id=where_is(other),
            device_id_type=MESH,
        )

    def chunk_step(chunk, carry):
        def grid_wait(k, inner):
            other = lax.rem(s + k, S)
            grid_copy(other, chunk, other).wait_recv()
            return inner

        lax.fori_loop(1, S, grid_wait, 0)
        for j in range(cp):
            plane = chunk * cp + j
            local_band = lax.rem(plane, nb)
            band = lax.rem(q0 + plane, B)
            value = grid[plane]
            for which in range(PASSES):
                index = which * nb + local_band
                mid = dot3((row_h[index], row_l[index]), split(value))
                blurred = dot3(split(mid), (col_h[index], col_l[index]))
                value = value + strength_ref[which, band] * (value - blurred)
            vh, vl = split(value)
            laid = dot3((place_h[0], place_l[0]), (vh[:, :BCOLS], vl[:, :BCOLS]))
            laid = laid + dot3((place_h[1], place_l[1]), (vh[:, BCOLS:], vl[:, BCOLS:]))
            asm[:, plane] = laid.reshape(n, share, BCOLS)

        def share_start(k, inner):
            share_copy(lax.rem(me + k, n), me, chunk).start()
            return inner

        lax.fori_loop(1, n, share_start, 0)
        return carry

    lax.fori_loop(0, nch, chunk_step, 0)
    stack[d, c, pl.ds(q0, ppd)] = asm[me]

    col_pair = split(cols_ref[...])

    def resample(source):
        sd = lax.rem(source // C, D)
        sc = lax.rem(source, C)
        ss = source // (D * C)
        block = stack[sd, sc, pl.ds(ss * ppd, ppd)].reshape(ppd * share, BCOLS)
        done = dot3(split(block), col_pair)
        stack[sd, sc, pl.ds(ss * ppd, ppd)] = done.reshape(ppd, share, BCOLS)

    resample(me)

    def share_wait(k, carry):
        source = lax.rem(me + n - k, n)

        def one(chunk, inner):
            share_copy(me, source, chunk).wait_recv()
            return inner

        lax.fori_loop(0, nch, one, 0)
        resample(source)
        return carry

    lax.fori_loop(1, n, share_wait, 0)

    count_sum = jnp.zeros((1, BCOLS), f32)
    for i in range(S * D):
        count_sum = count_sum + jnp.sum(meta_all[i, 8 : 8 + T, :BCOLS], axis=0, keepdims=True)
    mean_count = count_sum / (T * D * S)
    weights = []
    for i in range(D):
        mine = meta_all[s * D + i, 8 : 8 + T, :BCOLS]
        weights.append(mine / (mine + mean_count))

    step = 8 if share % 8 == 0 else share
    for start in range(0, share, step):

        def picked(i, t):
            return stack[i, :, t * B : (t + 1) * B, start : start + step, :]

        def weighted(estimate):
            num = jnp.zeros((C, B, step, BCOLS), f32)
            den = jnp.zeros((step, BCOLS), f32)
            for i in range(D):
                for t in range(T):
                    part = picked(i, t)
                    weight = jnp.broadcast_to(weights[i][t : t + 1], (step, BCOLS))
                    if estimate is not None:
                        away = part - estimate
                        square = jnp.sum(jnp.sum(away * away, axis=0), axis=0)
                        weight = weight * lax.rsqrt(square + smooth_sq)
                    num = num + weight * part
                    den = den + weight
            return num / den

        estimate = weighted(None)
        estimate = lax.fori_loop(0, ITERS, lambda _, e: weighted(e), estimate)
        est[:, :, start : start + step, :] = estimate

    def est_copy(other, source):
        return pltpu.make_async_remote_copy(
            src_ref=est.at[lax.rem(other, C)],
            dst_ref=res.at[source],
            send_sem=esend.at[other],
            recv_sem=erecv.at[source],
            device_id={"date": other // C, "band": lax.rem(other, C)},
            device_id_type=MESH,
        )

    def est_start(k, carry):
        est_copy(lax.rem(dc + k, D * C), dc).start()
        return carry

    lax.fori_loop(1, D * C, est_start, 0)
    res[dc] = est[c]

    def est_wait(k, carry):
        other = lax.rem(dc + k, D * C)
        copy = est_copy(other, other)
        copy.wait_send()
        copy.wait_recv()
        return carry

    lax.fori_loop(1, D * C, est_wait, 0)
    for i in range(D * C):
        out_ref[:, i * share : (i + 1) * share, :] = res[i]

    def chunk_end(chunk, carry):
        def grid_end(k, inner):
            grid_copy(lax.rem(s + k, S), chunk, s).wait_send()
            return inner

        def share_end(k, inner):
            share_copy(lax.rem(me + k, n), me, chunk).wait_send()
            return inner

        lax.fori_loop(1, S, grid_end, 0)
        lax.fori_loop(1, n, share_end, 0)
        return carry

    lax.fori_loop(0, nch, chunk_end, 0)


def local(
    reflect, kernels, strength, destinations, offsets, counts, resample_rows, resample_columns
):
    S, D, C = lax.axis_size("space"), lax.axis_size("date"), lax.axis_size("band")
    T, B, RS, W = reflect.shape
    PASSES, _, tap_count = kernels.shape
    radius = (tap_count - 1) // 2
    rows = S * RS
    n = S * D * C
    ppd = T * B // S
    nch = min(2, ppd)
    nb = min(B, ppd)
    tile_rows = destinations.shape[0] * BROWS
    share = tile_rows // (D * C)
    s = lax.axis_index("space")

    target = destinations[:, 0].reshape(-1, 2).T
    first = target * tile_rows + offsets.reshape(-1, 2).T
    places = jnp.repeat(jnp.concatenate([target, first]), BROWS, axis=1)
    strip = jnp.arange(rows)[None, :] // RS == s
    places = jnp.where(strip, jnp.tile(places, (1, S)), 0).astype(f32)
    tiled_rows = jnp.tile(resample_rows[0], (1, rows // BROWS))
    meta = jnp.concatenate(
        [places, tiled_rows, jnp.broadcast_to(counts.astype(f32), (T, rows))]
    )
    width = max(W, rows)
    taps = jnp.stack([kernels, kernels[:, :, ::-1]], axis=2).reshape(PASSES * B, 2, tap_count)
    taps = jnp.pad(taps, ((0, 0), (0, 0), (0, width - tap_count)))

    dims = (S, D, C, T, B, RS, W, PASSES, radius, ppd, nch)
    vmem = pl.BlockSpec(memory_space=pltpu.VMEM)
    smem = pl.BlockSpec(memory_space=pltpu.SMEM)
    dma = pltpu.SemaphoreType.DMA
    return pl.pallas_call(
        functools.partial(kernel, dims),
        out_shape=jax.ShapeDtypeStruct((B, tile_rows, BCOLS), f32),
        in_specs=[vmem, vmem, vmem, smem, vmem],
        out_specs=vmem,
        scratch_shapes=[
            pltpu.VMEM((ppd, rows, W), f32),
            pltpu.VMEM((PASSES * nb, rows, rows), bf16),
            pltpu.VMEM((PASSES * nb, rows, rows), bf16),
            pltpu.VMEM((PASSES * nb, W, W), bf16),
            pltpu.VMEM((PASSES * nb, W, W), bf16),
            pltpu.VMEM((S * D, 8 + T, rows), f32),
            pltpu.VMEM((2, S * tile_rows, rows), bf16),
            pltpu.VMEM((2, S * tile_rows, rows), bf16),
            pltpu.VMEM((n, ppd, share, BCOLS), f32),
            pltpu.VMEM((D, C, T * B, share, BCOLS), f32),
            pltpu.VMEM((C, B, share, BCOLS), f32),
            pltpu.VMEM((D * C, B, share, BCOLS), f32),
            dma((S * D,)),
            dma((S * D,)),
            dma((S, nch)),
            dma((S, nch)),
            dma((n, nch)),
            dma((n, nch)),
            dma((D * C,)),
            dma((D * C,)),
        ],
        compiler_params=pltpu.CompilerParams(
            collective_id=0, has_side_effects=True, vmem_limit_bytes=56 * 1024 * 1024
        ),
    )(reflect.reshape(T * B, RS, W), meta, taps, strength, resample_columns[0])


def solution(mesh):
    in_specs = (
        P("date", "band", ("groups", "space"), None),
        P(None, "band", None),
        P(None, "band"),
        P(("groups", "space"), None),
        P(("groups", "space")),
        P("date", ("groups", "space")),
        P(("groups", "space"), None, None),
        P(("groups", "space"), None, None),
    )
    out_specs = P("band", ("groups", "space"), None)
    return jax.shard_map(local, mesh=mesh, in_specs=in_specs, out_specs=out_specs, check_vma=False)
```

```python
import functools
import jax
import jax.numpy as jnp
from jax import lax
from jax.experimental import pallas as pl
from jax.experimental.pallas import tpu as pltpu
from jax.sharding import PartitionSpec as P

BROWS = 4
BCOLS = 128
ITERS = 4
MESH = pl.DeviceIdType.MESH
smooth_sq = 0.01
f32 = jnp.float32
bf16 = jnp.bfloat16


def split(value):
    high = value.astype(bf16)
    return high, (value - high.astype(f32)).astype(bf16)


def dot3(left, right):
    lh, ll = left
    rh, rl = right
    d = functools.partial(jnp.dot, preferred_element_type=f32)
    return d(lh, rh) + (d(ll, rh) + d(lh, rl))


def toeplitz(row, size, radius):
    base = jnp.broadcast_to(row, (8, size))
    base = pltpu.roll(base, size - radius, 1)
    sub = lax.broadcasted_iota(jnp.int32, (8, size), 0)
    for bit in (1, 2, 4):
        base = jnp.where((sub & bit) != 0, pltpu.roll(base, bit, 1), base)
    gap = lax.broadcasted_iota(jnp.int32, (8, size), 1) - sub
    parts = []
    for start in range(0, size, 8):
        turned = base if start == 0 else pltpu.roll(base, start, 1)
        near = jnp.abs(gap - start) <= radius
        parts.append(jnp.where(near, turned, 0.0))
    return jnp.concatenate(parts, axis=0)


def kernel(
    dims, x_ref, dest_ref, off_ref, counts_ref, rows_ref, taps_ref, strength_ref, cols_ref, out_ref,
    meta_ref, grid, row_h, row_l, col_h, col_l, meta_all, place_h, place_l, asm, stack, est, res,
    msend, mrecv, gsend, grecv, ssend, srecv, esend, erecv,
):
    S, D, C, T, B, RS, W, PASSES, radius, ppd, nch = dims
    n = S * D * C
    rows = S * RS
    nb = min(B, ppd)
    cp = ppd // nch
    share = asm.shape[2]
    s = lax.axis_index("space")
    d = lax.axis_index("date")
    c = lax.axis_index("band")
    me = (s * D + d) * C + c
    dc = d * C + c
    q0 = s * ppd

    def where_is(index):
        return {
            "space": index // (D * C),
            "date": lax.rem(index // C, D),
            "band": lax.rem(index, C),
        }

    barrier = pltpu.get_barrier_semaphore()

    def greet(k, carry):
        other = lax.rem(me + k, n)
        pl.semaphore_signal(barrier, inc=1, device_id=where_is(other), device_id_type=MESH)
        return carry

    lax.fori_loop(1, n, greet, 0)

    tile_rows = share * D * C
    lane = lax.broadcasted_iota(jnp.int32, (1, rows), 1)
    here = lax.div(lane, RS) == s
    row_block = lax.div(lax.rem(lane, RS), BROWS)
    count = off_ref.shape[0]
    for half in range(2):
        target = jnp.zeros((1, rows), jnp.int32)
        first = jnp.zeros((1, rows), jnp.int32)
        for j in range(half, count, 2):
            hit = here & (row_block == j // 2)
            target = jnp.where(hit, dest_ref[j, 0], target)
            first = jnp.where(hit, dest_ref[j, 0] * tile_rows + off_ref[j], first)
        meta_ref[half : half + 1, :] = target.astype(f32)
        meta_ref[2 + half : 3 + half, :] = first.astype(f32)
    for i in range(BROWS):
        value = jnp.zeros((1, rows), f32)
        for j in range(BROWS):
            value = jnp.where(lax.rem(lane, BROWS) == j, rows_ref[0, i, j], value)
        meta_ref[4 + i : 5 + i, :] = value
    for t in range(T):
        meta_ref[8 + t : 9 + t, :] = jnp.full((1, rows), counts_ref[t, 0], jnp.int32).astype(f32)

    pl.semaphore_wait(barrier, n - 1)

    md = s * D + d

    def meta_copy(to, slot, sem):
        return pltpu.make_async_remote_copy(
            src_ref=meta_ref,
            dst_ref=meta_all.at[slot],
            send_sem=msend.at[to],
            recv_sem=mrecv.at[sem],
            device_id={"space": to // D, "date": lax.rem(to, D)},
            device_id_type=MESH,
        )

    def meta_start(k, carry):
        meta_copy(lax.rem(md + k, S * D), md, md).start()
        return carry

    lax.fori_loop(1, S * D, meta_start, 0)
    meta_all[md] = meta_ref[...]

    def grid_copy(other, chunk, at):
        return pltpu.make_async_remote_copy(
            src_ref=x_ref.at[pl.ds(other * ppd + chunk * cp, cp)],
            dst_ref=grid.at[pl.ds(chunk * cp, cp), pl.ds(pl.multiple_of(at * RS, RS), RS)],
            send_sem=gsend.at[other, chunk],
            recv_sem=grecv.at[at, chunk],
            device_id={"space": other},
            device_id_type=MESH,
        )

    for chunk in range(nch):

        def grid_start(k, carry, chunk=chunk):
            grid_copy(lax.rem(s + k, S), chunk, s).start()
            return carry

        lax.fori_loop(1, S, grid_start, 0)
    grid[:, pl.ds(pl.multiple_of(s * RS, RS), RS), :] = x_ref[pl.ds(q0, ppd)]

    def build(index, carry):
        which = index // nb
        local_band = lax.rem(index, nb)
        band = lax.rem(q0 + local_band, B)
        both = taps_ref[which * B + band]
        both = both / jnp.sum(both, axis=1, keepdims=True)
        high, low = split(toeplitz(both[0:1, :rows], rows, radius))
        row_h[index] = high
        row_l[index] = low
        high, low = split(toeplitz(both[1:2, :W], W, radius))
        col_h[index] = high
        col_l[index] = low
        return carry

    lax.fori_loop(0, PASSES * nb, build, 0)

    def meta_wait(k, carry):
        other = lax.rem(md + k, S * D)
        copy = meta_copy(other, other, other)
        copy.wait_send()
        copy.wait_recv()
        return carry

    lax.fori_loop(1, S * D, meta_wait, 0)

    pieces = [meta_all[i * D + d, 0:8, :] for i in range(S)]
    total = pieces[0]
    for piece in pieces[1:]:
        total = total + piece
    map_row = lax.broadcasted_iota(jnp.int32, (S * tile_rows, rows), 0)
    for half in range(2):
        target = total[half : half + 1]
        first = total[2 + half : 3 + half].astype(jnp.int32)
        behind = map_row - first
        place = jnp.zeros((S * tile_rows, rows), f32)
        for i in range(BROWS):
            value = jnp.zeros((1, rows), f32)
            for tile in range(S):
                value = value + jnp.where(target == tile, pieces[tile][4 + i : 5 + i], 0.0)
            place = jnp.where(behind == i, value, place)
        high, low = split(place)
        place_h[half] = high
        place_l[half] = low

    def share_copy(other, source, chunk):
        sd = lax.rem(source // C, D)
        sc = lax.rem(source, C)
        ss = source // (D * C)
        return pltpu.make_async_remote_copy(
            src_ref=asm.at[other, pl.ds(chunk * cp, cp)],
            dst_ref=stack.at[sd, sc, pl.ds(ss * ppd + chunk * cp, cp)],
            send_sem=ssend.at[other, chunk],
            recv_sem=srecv.at[source, chunk],
            device_id=where_is(other),
            device_id_type=MESH,
        )

    def chunk_step(chunk, carry):
        def grid_wait(k, inner):
            other = lax.rem(s + k, S)
            grid_copy(other, chunk, other).wait_recv()
            return inner

        lax.fori_loop(1, S, grid_wait, 0)
        for j in range(cp):
            plane = chunk * cp + j
            local_band = lax.rem(plane, nb)
            band = lax.rem(q0 + plane, B)
            value = grid[plane]
            for which in range(PASSES):
                index = which * nb + local_band
                mid = dot3((row_h[index], row_l[index]), split(value))
                blurred = dot3(split(mid), (col_h[index], col_l[index]))
                value = value + strength_ref[which, band] * (value - blurred)
            vh, vl = split(value)
            laid = dot3((place_h[0], place_l[0]), (vh[:, :BCOLS], vl[:, :BCOLS]))
            laid = laid + dot3((place_h[1], place_l[1]), (vh[:, BCOLS:], vl[:, BCOLS:]))
            asm[:, plane] = laid.reshape(n, share, BCOLS)

        def share_start(k, inner):
            share_copy(lax.rem(me + k, n), me, chunk).start()
            return inner

        lax.fori_loop(1, n, share_start, 0)
        return carry

    lax.fori_loop(0, nch, chunk_step, 0)
    stack[d, c, pl.ds(q0, ppd)] = asm[me]

    col_pair = split(cols_ref[...])

    def resample(source):
        sd = lax.rem(source // C, D)
        sc = lax.rem(source, C)
        ss = source // (D * C)
        block = stack[sd, sc, pl.ds(ss * ppd, ppd)].reshape(ppd * share, BCOLS)
        done = dot3(split(block), col_pair)
        stack[sd, sc, pl.ds(ss * ppd, ppd)] = done.reshape(ppd, share, BCOLS)

    resample(me)

    def share_wait(k, carry):
        source = lax.rem(me + n - k, n)

        def one(chunk, inner):
            share_copy(me, source, chunk).wait_recv()
            return inner

        lax.fori_loop(0, nch, one, 0)
        resample(source)
        return carry

    lax.fori_loop(1, n, share_wait, 0)

    count_sum = jnp.zeros((1, BCOLS), f32)
    for i in range(S * D):
        count_sum = count_sum + jnp.sum(meta_all[i, 8 : 8 + T, :BCOLS], axis=0, keepdims=True)
    mean_count = count_sum / (T * D * S)
    weights = []
    for i in range(D):
        mine = meta_all[s * D + i, 8 : 8 + T, :BCOLS]
        weights.append(mine / (mine + mean_count))

    step = 8 if share % 8 == 0 else share
    for start in range(0, share, step):

        def picked(i, t):
            return stack[i, :, t * B : (t + 1) * B, start : start + step, :]

        def weighted(estimate):
            num = jnp.zeros((C, B, step, BCOLS), f32)
            den = jnp.zeros((step, BCOLS), f32)
            for i in range(D):
                for t in range(T):
                    part = picked(i, t)
                    weight = jnp.broadcast_to(weights[i][t : t + 1], (step, BCOLS))
                    if estimate is not None:
                        away = part - estimate
                        square = jnp.sum(jnp.sum(away * away, axis=0), axis=0)
                        weight = weight * lax.rsqrt(square + smooth_sq)
                    num = num + weight * part
                    den = den + weight
            return num / den

        estimate = weighted(None)
        estimate = lax.fori_loop(0, ITERS, lambda _, e: weighted(e), estimate)
        est[:, :, start : start + step, :] = estimate

    def est_copy(other, source):
        return pltpu.make_async_remote_copy(
            src_ref=est.at[lax.rem(other, C)],
            dst_ref=res.at[source],
            send_sem=esend.at[other],
            recv_sem=erecv.at[source],
            device_id={"date": other // C, "band": lax.rem(other, C)},
            device_id_type=MESH,
        )

    def est_start(k, carry):
        est_copy(lax.rem(dc + k, D * C), dc).start()
        return carry

    lax.fori_loop(1, D * C, est_start, 0)
    res[dc] = est[c]

    def est_wait(k, carry):
        other = lax.rem(dc + k, D * C)
        copy = est_copy(other, other)
        copy.wait_send()
        copy.wait_recv()
        return carry

    lax.fori_loop(1, D * C, est_wait, 0)
    for i in range(D * C):
        out_ref[:, i * share : (i + 1) * share, :] = res[i]

    def chunk_end(chunk, carry):
        def grid_end(k, inner):
            grid_copy(lax.rem(s + k, S), chunk, s).wait_send()
            return inner

        def share_end(k, inner):
            share_copy(lax.rem(me + k, n), me, chunk).wait_send()
            return inner

        lax.fori_loop(1, S, grid_end, 0)
        lax.fori_loop(1, n, share_end, 0)
        return carry

    lax.fori_loop(0, nch, chunk_end, 0)


def local(
    reflect, kernels, strength, destinations, offsets, counts, resample_rows, resample_columns
):
    S, D, C = lax.axis_size("space"), lax.axis_size("date"), lax.axis_size("band")
    T, B, RS, W = reflect.shape
    PASSES, _, tap_count = kernels.shape
    radius = (tap_count - 1) // 2
    rows = S * RS
    n = S * D * C
    ppd = T * B // S
    nch = min(2, ppd)
    nb = min(B, ppd)
    tile_rows = destinations.shape[0] * BROWS
    share = tile_rows // (D * C)
    width = max(W, rows)
    taps = jnp.stack([kernels, kernels[:, :, ::-1]], axis=2).reshape(PASSES * B, 2, tap_count)
    taps = jnp.pad(taps, ((0, 0), (0, 0), (0, width - tap_count)))

    dims = (S, D, C, T, B, RS, W, PASSES, radius, ppd, nch)
    vmem = pl.BlockSpec(memory_space=pltpu.VMEM)
    smem = pl.BlockSpec(memory_space=pltpu.SMEM)
    dma = pltpu.SemaphoreType.DMA
    return pl.pallas_call(
        functools.partial(kernel, dims),
        out_shape=jax.ShapeDtypeStruct((B, tile_rows, BCOLS), f32),
        in_specs=[vmem, smem, smem, smem, smem, vmem, smem, vmem],
        out_specs=vmem,
        scratch_shapes=[
            pltpu.VMEM((8 + T, rows), f32),
            pltpu.VMEM((ppd, rows, W), f32),
            pltpu.VMEM((PASSES * nb, rows, rows), bf16),
            pltpu.VMEM((PASSES * nb, rows, rows), bf16),
            pltpu.VMEM((PASSES * nb, W, W), bf16),
            pltpu.VMEM((PASSES * nb, W, W), bf16),
            pltpu.VMEM((S * D, 8 + T, rows), f32),
            pltpu.VMEM((2, S * tile_rows, rows), bf16),
            pltpu.VMEM((2, S * tile_rows, rows), bf16),
            pltpu.VMEM((n, ppd, share, BCOLS), f32),
            pltpu.VMEM((D, C, T * B, share, BCOLS), f32),
            pltpu.VMEM((C, B, share, BCOLS), f32),
            pltpu.VMEM((D * C, B, share, BCOLS), f32),
            dma((S * D,)),
            dma((S * D,)),
            dma((S, nch)),
            dma((S, nch)),
            dma((n, nch)),
            dma((n, nch)),
            dma((D * C,)),
            dma((D * C,)),
        ],
        compiler_params=pltpu.CompilerParams(
            collective_id=0, has_side_effects=True, vmem_limit_bytes=56 * 1024 * 1024
        ),
    )(reflect.reshape(T * B, RS, W), destinations, offsets, counts, resample_rows, taps, strength, resample_columns[0])


def solution(mesh):
    in_specs = (
        P("date", "band", ("groups", "space"), None),
        P(None, "band", None),
        P(None, "band"),
        P(("groups", "space"), None),
        P(("groups", "space")),
        P("date", ("groups", "space")),
        P(("groups", "space"), None, None),
        P(("groups", "space"), None, None),
    )
    out_specs = P("band", ("groups", "space"), None)
    return jax.shard_map(local, mesh=mesh, in_specs=in_specs, out_specs=out_specs, check_vma=False)
```

```python
import functools
import jax
import jax.numpy as jnp
from jax import lax
from jax.experimental import pallas as pl
from jax.experimental.pallas import tpu as pltpu
from jax.sharding import PartitionSpec as P

BROWS = 4
BCOLS = 128
ITERS = 4
MESH = pl.DeviceIdType.MESH
smooth_sq = 0.01
f32 = jnp.float32
bf16 = jnp.bfloat16


def split(value):
    high = value.astype(bf16)
    return high, (value - high.astype(f32)).astype(bf16)


def dot3(left, right):
    lh, ll = left
    rh, rl = right
    d = functools.partial(jnp.dot, preferred_element_type=f32)
    return d(lh, rh) + (d(ll, rh) + d(lh, rl))


def toeplitz(row, size, radius):
    base = jnp.broadcast_to(row, (8, size))
    base = pltpu.roll(base, size - radius, 1)
    sub = lax.broadcasted_iota(jnp.int32, (8, size), 0)
    for bit in (1, 2, 4):
        base = jnp.where((sub & bit) != 0, pltpu.roll(base, bit, 1), base)
    gap = lax.broadcasted_iota(jnp.int32, (8, size), 1) - sub
    parts = []
    for start in range(0, size, 8):
        turned = base if start == 0 else pltpu.roll(base, start, 1)
        near = jnp.abs(gap - start) <= radius
        parts.append(jnp.where(near, turned, 0.0))
    return jnp.concatenate(parts, axis=0)


def kernel(
    dims, x_ref, dest_ref, off_ref, counts_ref, rows_ref, taps_ref, strength_ref, cols_ref, out_ref,
    meta_ref, grid, row_h, row_l, col_h, col_l, meta_all, place_h, place_l, asm, stack, est, res,
    msend, mrecv, gsend, grecv, ssend, srecv, esend, erecv,
):
    S, D, C, T, B, RS, W, PASSES, radius, ppd, nch = dims
    n = S * D * C
    rows = S * RS
    nb = min(B, ppd)
    cp = ppd // nch
    share = asm.shape[2]
    s = lax.axis_index("space")
    d = lax.axis_index("date")
    c = lax.axis_index("band")
    me = (s * D + d) * C + c
    dc = d * C + c
    q0 = s * ppd

    def where_is(index):
        return {
            "space": index // (D * C),
            "date": lax.rem(index // C, D),
            "band": lax.rem(index, C),
        }

    barrier = pltpu.get_barrier_semaphore()

    def greet(k, carry):
        other = lax.rem(me + k, n)
        pl.semaphore_signal(barrier, inc=1, device_id=where_is(other), device_id_type=MESH)
        return carry

    lax.fori_loop(1, n, greet, 0)

    tile_rows = share * D * C
    lane = lax.broadcasted_iota(jnp.int32, (1, rows), 1)
    here = lax.div(lane, RS) == s
    row_block = lax.div(lax.rem(lane, RS), BROWS)
    count = off_ref.shape[0]
    for half in range(2):
        target = jnp.zeros((1, rows), jnp.int32)
        first = jnp.zeros((1, rows), jnp.int32)
        for j in range(half, count, 2):
            hit = here & (row_block == j // 2)
            target = jnp.where(hit, dest_ref[j], target)
            first = jnp.where(hit, dest_ref[j] * tile_rows + off_ref[j], first)
        meta_ref[half : half + 1, :] = target.astype(f32)
        meta_ref[2 + half : 3 + half, :] = first.astype(f32)
    for i in range(BROWS):
        value = jnp.zeros((1, rows), f32)
        for j in range(BROWS):
            value = jnp.where(lax.rem(lane, BROWS) == j, rows_ref[0, i, j], value)
        meta_ref[4 + i : 5 + i, :] = value
    for t in range(T):
        meta_ref[8 + t : 9 + t, :] = jnp.full((1, rows), counts_ref[t], jnp.int32).astype(f32)

    pl.semaphore_wait(barrier, n - 1)

    md = s * D + d

    def meta_copy(to, slot, sem):
        return pltpu.make_async_remote_copy(
            src_ref=meta_ref,
            dst_ref=meta_all.at[slot],
            send_sem=msend.at[to],
            recv_sem=mrecv.at[sem],
            device_id={"space": to // D, "date": lax.rem(to, D)},
            device_id_type=MESH,
        )

    def meta_start(k, carry):
        meta_copy(lax.rem(md + k, S * D), md, md).start()
        return carry

    lax.fori_loop(1, S * D, meta_start, 0)
    meta_all[md] = meta_ref[...]

    def grid_copy(other, chunk, at):
        return pltpu.make_async_remote_copy(
            src_ref=x_ref.at[pl.ds(other * ppd + chunk * cp, cp)],
            dst_ref=grid.at[pl.ds(chunk * cp, cp), pl.ds(pl.multiple_of(at * RS, RS), RS)],
            send_sem=gsend.at[other, chunk],
            recv_sem=grecv.at[at, chunk],
            device_id={"space": other},
            device_id_type=MESH,
        )

    for chunk in range(nch):

        def grid_start(k, carry, chunk=chunk):
            grid_copy(lax.rem(s + k, S), chunk, s).start()
            return carry

        lax.fori_loop(1, S, grid_start, 0)
    grid[:, pl.ds(pl.multiple_of(s * RS, RS), RS), :] = x_ref[pl.ds(q0, ppd)]

    def build(index, carry):
        which = index // nb
        local_band = lax.rem(index, nb)
        band = lax.rem(q0 + local_band, B)
        both = taps_ref[which * B + band]
        both = both / jnp.sum(both, axis=1, keepdims=True)
        high, low = split(toeplitz(both[0:1, :rows], rows, radius))
        row_h[index] = high
        row_l[index] = low
        high, low = split(toeplitz(both[1:2, :W], W, radius))
        col_h[index] = high
        col_l[index] = low
        return carry

    lax.fori_loop(0, PASSES * nb, build, 0)

    def meta_wait(k, carry):
        other = lax.rem(md + k, S * D)
        copy = meta_copy(other, other, other)
        copy.wait_send()
        copy.wait_recv()
        return carry

    lax.fori_loop(1, S * D, meta_wait, 0)

    pieces = [meta_all[i * D + d, 0:8, :] for i in range(S)]
    total = pieces[0]
    for piece in pieces[1:]:
        total = total + piece
    map_row = lax.broadcasted_iota(jnp.int32, (S * tile_rows, rows), 0)
    for half in range(2):
        target = total[half : half + 1]
        first = total[2 + half : 3 + half].astype(jnp.int32)
        behind = map_row - first
        place = jnp.zeros((S * tile_rows, rows), f32)
        for i in range(BROWS):
            value = jnp.zeros((1, rows), f32)
            for tile in range(S):
                value = value + jnp.where(target == tile, pieces[tile][4 + i : 5 + i], 0.0)
            place = jnp.where(behind == i, value, place)
        high, low = split(place)
        place_h[half] = high
        place_l[half] = low

    def share_copy(other, source, chunk):
        sd = lax.rem(source // C, D)
        sc = lax.rem(source, C)
        ss = source // (D * C)
        return pltpu.make_async_remote_copy(
            src_ref=asm.at[other, pl.ds(chunk * cp, cp)],
            dst_ref=stack.at[sd, sc, pl.ds(ss * ppd + chunk * cp, cp)],
            send_sem=ssend.at[other, chunk],
            recv_sem=srecv.at[source, chunk],
            device_id=where_is(other),
            device_id_type=MESH,
        )

    def chunk_step(chunk, carry):
        def grid_wait(k, inner):
            other = lax.rem(s + k, S)
            grid_copy(other, chunk, other).wait_recv()
            return inner

        lax.fori_loop(1, S, grid_wait, 0)
        for j in range(cp):
            plane = chunk * cp + j
            local_band = lax.rem(plane, nb)
            band = lax.rem(q0 + plane, B)
            value = grid[plane]
            for which in range(PASSES):
                index = which * nb + local_band
                mid = dot3((row_h[index], row_l[index]), split(value))
                blurred = dot3(split(mid), (col_h[index], col_l[index]))
                value = value + strength_ref[which, band] * (value - blurred)
            vh, vl = split(value)
            laid = dot3((place_h[0], place_l[0]), (vh[:, :BCOLS], vl[:, :BCOLS]))
            laid = laid + dot3((place_h[1], place_l[1]), (vh[:, BCOLS:], vl[:, BCOLS:]))
            asm[:, plane] = laid.reshape(n, share, BCOLS)

        def share_start(k, inner):
            share_copy(lax.rem(me + k, n), me, chunk).start()
            return inner

        lax.fori_loop(1, n, share_start, 0)
        return carry

    lax.fori_loop(0, nch, chunk_step, 0)
    stack[d, c, pl.ds(q0, ppd)] = asm[me]

    col_pair = split(cols_ref[...])

    def resample(source):
        sd = lax.rem(source // C, D)
        sc = lax.rem(source, C)
        ss = source // (D * C)
        block = stack[sd, sc, pl.ds(ss * ppd, ppd)].reshape(ppd * share, BCOLS)
        done = dot3(split(block), col_pair)
        stack[sd, sc, pl.ds(ss * ppd, ppd)] = done.reshape(ppd, share, BCOLS)

    resample(me)

    def share_wait(k, carry):
        source = lax.rem(me + n - k, n)

        def one(chunk, inner):
            share_copy(me, source, chunk).wait_recv()
            return inner

        lax.fori_loop(0, nch, one, 0)
        resample(source)
        return carry

    lax.fori_loop(1, n, share_wait, 0)

    count_sum = jnp.zeros((1, BCOLS), f32)
    for i in range(S * D):
        count_sum = count_sum + jnp.sum(meta_all[i, 8 : 8 + T, :BCOLS], axis=0, keepdims=True)
    mean_count = count_sum / (T * D * S)
    weights = []
    for i in range(D):
        mine = meta_all[s * D + i, 8 : 8 + T, :BCOLS]
        weights.append(mine / (mine + mean_count))

    step = 8 if share % 8 == 0 else share
    for start in range(0, share, step):

        def picked(i, t):
            return stack[i, :, t * B : (t + 1) * B, start : start + step, :]

        def weighted(estimate):
            num = jnp.zeros((C, B, step, BCOLS), f32)
            den = jnp.zeros((step, BCOLS), f32)
            for i in range(D):
                for t in range(T):
                    part = picked(i, t)
                    weight = jnp.broadcast_to(weights[i][t : t + 1], (step, BCOLS))
                    if estimate is not None:
                        away = part - estimate
                        square = jnp.sum(jnp.sum(away * away, axis=0), axis=0)
                        weight = weight * lax.rsqrt(square + smooth_sq)
                    num = num + weight * part
                    den = den + weight
            return num / den

        estimate = weighted(None)
        estimate = lax.fori_loop(0, ITERS, lambda _, e: weighted(e), estimate)
        est[:, :, start : start + step, :] = estimate

    def est_copy(other, source):
        return pltpu.make_async_remote_copy(
            src_ref=est.at[lax.rem(other, C)],
            dst_ref=res.at[source],
            send_sem=esend.at[other],
            recv_sem=erecv.at[source],
            device_id={"date": other // C, "band": lax.rem(other, C)},
            device_id_type=MESH,
        )

    def est_start(k, carry):
        est_copy(lax.rem(dc + k, D * C), dc).start()
        return carry

    lax.fori_loop(1, D * C, est_start, 0)
    res[dc] = est[c]

    def est_wait(k, carry):
        other = lax.rem(dc + k, D * C)
        copy = est_copy(other, other)
        copy.wait_send()
        copy.wait_recv()
        return carry

    lax.fori_loop(1, D * C, est_wait, 0)
    for i in range(D * C):
        out_ref[:, i * share : (i + 1) * share, :] = res[i]

    def chunk_end(chunk, carry):
        def grid_end(k, inner):
            grid_copy(lax.rem(s + k, S), chunk, s).wait_send()
            return inner

        def share_end(k, inner):
            share_copy(lax.rem(me + k, n), me, chunk).wait_send()
            return inner

        lax.fori_loop(1, S, grid_end, 0)
        lax.fori_loop(1, n, share_end, 0)
        return carry

    lax.fori_loop(0, nch, chunk_end, 0)


def local(
    reflect, kernels, strength, destinations, offsets, counts, resample_rows, resample_columns
):
    S, D, C = lax.axis_size("space"), lax.axis_size("date"), lax.axis_size("band")
    T, B, RS, W = reflect.shape
    PASSES, _, tap_count = kernels.shape
    radius = (tap_count - 1) // 2
    rows = S * RS
    n = S * D * C
    ppd = T * B // S
    nch = min(2, ppd)
    nb = min(B, ppd)
    tile_rows = destinations.shape[0] * BROWS
    share = tile_rows // (D * C)
    width = max(W, rows)
    taps = jnp.stack([kernels, kernels[:, :, ::-1]], axis=2).reshape(PASSES * B, 2, tap_count)
    taps = jnp.pad(taps, ((0, 0), (0, 0), (0, width - tap_count)))

    dims = (S, D, C, T, B, RS, W, PASSES, radius, ppd, nch)
    vmem = pl.BlockSpec(memory_space=pltpu.VMEM)
    smem = pl.BlockSpec(memory_space=pltpu.SMEM)
    dma = pltpu.SemaphoreType.DMA
    return pl.pallas_call(
        functools.partial(kernel, dims),
        out_shape=jax.ShapeDtypeStruct((B, tile_rows, BCOLS), f32),
        in_specs=[vmem, smem, smem, smem, smem, vmem, smem, vmem],
        out_specs=vmem,
        scratch_shapes=[
            pltpu.VMEM((8 + T, rows), f32),
            pltpu.VMEM((ppd, rows, W), f32),
            pltpu.VMEM((PASSES * nb, rows, rows), bf16),
            pltpu.VMEM((PASSES * nb, rows, rows), bf16),
            pltpu.VMEM((PASSES * nb, W, W), bf16),
            pltpu.VMEM((PASSES * nb, W, W), bf16),
            pltpu.VMEM((S * D, 8 + T, rows), f32),
            pltpu.VMEM((2, S * tile_rows, rows), bf16),
            pltpu.VMEM((2, S * tile_rows, rows), bf16),
            pltpu.VMEM((n, ppd, share, BCOLS), f32),
            pltpu.VMEM((D, C, T * B, share, BCOLS), f32),
            pltpu.VMEM((C, B, share, BCOLS), f32),
            pltpu.VMEM((D * C, B, share, BCOLS), f32),
            dma((S * D,)),
            dma((S * D,)),
            dma((S, nch)),
            dma((S, nch)),
            dma((n, nch)),
            dma((n, nch)),
            dma((D * C,)),
            dma((D * C,)),
        ],
        compiler_params=pltpu.CompilerParams(
            collective_id=0, has_side_effects=True, vmem_limit_bytes=56 * 1024 * 1024
        ),
    )(reflect.reshape(T * B, RS, W), destinations[:, 0], offsets, counts[:, 0], resample_rows, taps, strength, resample_columns[0])


def solution(mesh):
    in_specs = (
        P("date", "band", ("groups", "space"), None),
        P(None, "band", None),
        P(None, "band"),
        P(("groups", "space"), None),
        P(("groups", "space")),
        P("date", ("groups", "space")),
        P(("groups", "space"), None, None),
        P(("groups", "space"), None, None),
    )
    out_specs = P("band", ("groups", "space"), None)
    return jax.shard_map(local, mesh=mesh, in_specs=in_specs, out_specs=out_specs, check_vma=False)
```
